512 devices in a mesh: dp: 16 (over z, core), seq: 32 (over x, y).
Axes of the slice: x: 4, y: 8, z: 8, core: 2. Of those that a mesh axis runs over, the one named last changes fastest.
Arguments:
- queries: bfloat16 [65536, 4096], P(('dp', 'seq')), may hold values from -6 to 6
- keys: bfloat16 [65536, 512], P(('dp', 'seq')), may hold values from -6 to 6
- values: bfloat16 [65536, 512], P(('dp', 'seq')), may hold values from -6 to 6
- d_out: bfloat16 [65536, 4096], P(('dp', 'seq')), may hold values from -6 to 6
- doc_lengths: int32 [171], replicated, may hold values from 1 to 768, as said below
Outputs:
- d_queries: bfloat16 [65536, 4096], P(('dp', 'seq'))
- key_gradient: bfloat16 [65536, 512], P(('dp', 'seq'))
- value_gradient: bfloat16 [65536, 512], P(('dp', 'seq'))
The draws below stay inside these ranges and needn't reach their ends.
Inputs may be any that keep to these rules, and one draw needn't show every extreme that they name: `doc_lengths`: lengths of the 171 documents in order; they sum to 65536, and the longest has exactly 768 tokens.
All inputs are finite; a program needn't handle non-finite values.
Results may differ from the reference program's by a relative error of at most 0.008.
Values may be sent and summed in bfloat16 or wider, within the bound.
A program may use at most 64 MiB of HBM per device.

```python
import math
import jax
import jax.numpy as jnp
from jax import lax

HEAD_SIZE = 128
GROUP = 8
DOC_MOST = 768
HQ = 32
KEY_VALUE_HEADS = 4
PACKED_TOKENS = 65536
NDOC = 171


def lengths_from(key):
    others_count = NDOC - 1
    leftover = PACKED_TOKENS - DOC_MOST - others_count
    middle = leftover // others_count
    surplus = leftover % others_count
    spread_max = min(middle, DOC_MOST - 2 - middle)
    shifts = jax.random.randint(jax.random.fold_in(key, 11), (others_count // 2,), -spread_max, spread_max + 1, dtype=jnp.int32)
    pieces = jnp.concatenate([shifts, -shifts])
    bumped = (jnp.arange(others_count, dtype=jnp.int32) < surplus).astype(jnp.int32)
    others = 1 + middle + pieces + bumped
    all_lengths = jnp.concatenate([jnp.full((1,), DOC_MOST, jnp.int32), others])
    shuffle = jax.random.permutation(jax.random.fold_in(key, 12), NDOC)
    return all_lengths[shuffle]


def draw_doc_lengths(key, part):
    return lengths_from(key)


def draw_keys(key, part):
    sampled_draw = jnp.clip(jax.random.normal(jax.random.fold_in(key, 22), (PACKED_TOKENS, KEY_VALUE_HEADS, HEAD_SIZE), jnp.float32), -6.0, 6.0)
    return sampled_draw.reshape(PACKED_TOKENS, KEY_VALUE_HEADS * HEAD_SIZE).astype(jnp.bfloat16)


def draw_queries(key, part):
    sampled_draw = jnp.clip(jax.random.normal(jax.random.fold_in(key, 21), (PACKED_TOKENS, HQ, HEAD_SIZE), jnp.float32), -6.0, 6.0)
    return sampled_draw.reshape(PACKED_TOKENS, HQ * HEAD_SIZE).astype(jnp.bfloat16)


def block_scale(rng, shape, split, least, high):
    gain, own = 1.0, jax.random.fold_in(rng, 6)
    for dim, shards_of in split:
        steps = jnp.exp(jax.random.uniform(jax.random.fold_in(own, dim), (shards_of,), jnp.float32, least / len(split), high / len(split)))
        gain = gain * jnp.repeat(steps, shape[dim] // shards_of).reshape([-1 if axis == dim else 1 for axis in range(len(shape))])
    return gain


def scatter_about(rng, extent, width, most, cuts=(), held_as=jnp.bfloat16):
    loudness = block_scale(rng, extent, cuts, -0.22, 0.18) if cuts else 1.0
    result = jax.random.normal(rng, extent, jnp.float32) * width * loudness
    return jnp.minimum(jnp.maximum(result, -most), most).astype(held_as)


def setup_inputs(seed: int = 0) -> dict:
    splits = jax.random.split(jax.random.key(seed), 6)
    return {
        "queries": draw_queries(jax.random.fold_in(splits[5], 71), 0),
        "keys": draw_keys(jax.random.fold_in(splits[5], 71), 0),
        "values": scatter_about(splits[2], (PACKED_TOKENS, KEY_VALUE_HEADS * HEAD_SIZE), 1.0, 6.0, ((0, 512),)),
        "d_out": scatter_about(splits[3], (PACKED_TOKENS, HQ * HEAD_SIZE), 1.0, 6.0, ((0, 512),)),
        "doc_lengths": draw_doc_lengths(jax.random.fold_in(splits[5], 71), 0),
    }


def doc_index(positions, doc_ends):
    return lax.optimization_barrier(jnp.sum((positions[:, None] >= doc_ends[None, :]).astype(jnp.int32), axis=1))

def block_grads(q_rows, key_rows, value_rows, grad_rows, allowed, score_scale):
    scores = jnp.dot(q_rows, key_rows.T, preferred_element_type=jnp.float32) * score_scale
    scores = jnp.where(allowed, scores, -1e+30)
    row_max = lax.optimization_barrier(jnp.max(scores, axis=1, keepdims=True))
    exp_scores = jnp.exp(scores - row_max)
    attn_probs = exp_scores / lax.optimization_barrier(jnp.sum(exp_scores, axis=1, keepdims=True))
    probs_low = attn_probs.astype(jnp.bfloat16)
    grad_probs = jnp.dot(grad_rows, value_rows.T, preferred_element_type=jnp.float32)
    row_delta = lax.optimization_barrier(jnp.sum(attn_probs * grad_probs, axis=1, keepdims=True))
    grad_scores = (attn_probs * (grad_probs - row_delta) * score_scale).astype(jnp.bfloat16)
    grad_q = jnp.dot(grad_scores, key_rows, preferred_element_type=jnp.float32)
    grad_k = jnp.dot(grad_scores.T, q_rows, preferred_element_type=jnp.float32)
    grad_v = jnp.dot(probs_low.T, grad_rows, preferred_element_type=jnp.float32)
    return (grad_q, grad_k, grad_v)

def reference(queries, keys, values, d_out, doc_lengths):
    grand_total = queries.shape[0]
    doc_ends = jnp.cumsum(doc_lengths).astype(jnp.int32)
    query_span = min(512, grand_total)
    key_window = min(query_span + DOC_MOST, grand_total)
    steps_count = grand_total // query_span
    positions = jnp.arange(grand_total, dtype=jnp.int32)
    all_docs = doc_index(positions, doc_ends)
    q_heads = queries.reshape(grand_total, HQ, HEAD_SIZE)
    g_heads = d_out.reshape(grand_total, HQ, HEAD_SIZE)
    key_head_list = keys.reshape(grand_total, KEY_VALUE_HEADS, HEAD_SIZE)
    value_head_list = values.reshape(grand_total, KEY_VALUE_HEADS, HEAD_SIZE)
    score_scale = 1.0 / math.sqrt(HEAD_SIZE)

    def one_head(sums, head_index):
        key_sum_total, value_sum_total = sums
        q_head = lax.dynamic_index_in_dim(q_heads, head_index, 1, keepdims=False)
        g_head = lax.dynamic_index_in_dim(g_heads, head_index, 1, keepdims=False)
        kv_index = (head_index // GROUP).astype(jnp.int32)
        k_head = lax.dynamic_index_in_dim(key_head_list, kv_index, 1, keepdims=False)
        v_head = lax.dynamic_index_in_dim(value_head_list, kv_index, 1, keepdims=False)

        def step(totals, step_index):
            acc_k, acc_v = totals
            row_start = (step_index * query_span).astype(jnp.int32)
            key_start = jnp.clip(row_start - DOC_MOST, 0, grand_total - key_window).astype(jnp.int32)
            q_rows = lax.dynamic_slice_in_dim(q_head, row_start, query_span, 0)
            g_rows = lax.dynamic_slice_in_dim(g_head, row_start, query_span, 0)
            key_rows = lax.dynamic_slice_in_dim(k_head, key_start, key_window, 0)
            value_rows = lax.dynamic_slice_in_dim(v_head, key_start, key_window, 0)
            q_pos = lax.dynamic_slice_in_dim(positions, row_start, query_span, 0)
            k_pos = lax.dynamic_slice_in_dim(positions, key_start, key_window, 0)
            q_docs = lax.dynamic_slice_in_dim(all_docs, row_start, query_span, 0)
            k_docs = lax.dynamic_slice_in_dim(all_docs, key_start, key_window, 0)
            allowed = (q_docs[:, None] == k_docs[None, :]) & (k_pos[None, :] <= q_pos[:, None])
            grad_q, grad_k, grad_v = block_grads(q_rows, key_rows, value_rows, g_rows, allowed, score_scale)
            acc_k = lax.dynamic_update_slice_in_dim(acc_k, lax.dynamic_slice_in_dim(acc_k, key_start, key_window, 0) + grad_k, key_start, 0)
            acc_v = lax.dynamic_update_slice_in_dim(acc_v, lax.dynamic_slice_in_dim(acc_v, key_start, key_window, 0) + grad_v, key_start, 0)
            return ((acc_k, acc_v), grad_q.astype(jnp.bfloat16))
        empty_acc = jnp.zeros((grand_total, HEAD_SIZE), jnp.float32)
        (acc_k, acc_v), q_blocks = lax.scan(step, (empty_acc, empty_acc), jnp.arange(steps_count, dtype=jnp.int32))
        key_sum_total = key_sum_total.at[kv_index].add(acc_k)
        value_sum_total = value_sum_total.at[kv_index].add(acc_v)
        return ((key_sum_total, value_sum_total), q_blocks.reshape(grand_total, HEAD_SIZE))
    initial_sum = jnp.zeros((KEY_VALUE_HEADS, grand_total, HEAD_SIZE), jnp.float32)
    (key_sum_total, value_sum_total), grad_q = lax.scan(one_head, (initial_sum, initial_sum), jnp.arange(HQ, dtype=jnp.int32))
    d_queries = jnp.transpose(grad_q, (1, 0, 2)).reshape(grand_total, HQ * HEAD_SIZE)
    key_gradient = jnp.transpose(key_sum_total, (1, 0, 2)).reshape(grand_total, KEY_VALUE_HEADS * HEAD_SIZE).astype(jnp.bfloat16)
    value_gradient = jnp.transpose(value_sum_total, (1, 0, 2)).reshape(grand_total, KEY_VALUE_HEADS * HEAD_SIZE).astype(jnp.bfloat16)
    return (d_queries, key_gradient, value_gradient)
```

```python
import functools
import math

import jax
import jax.numpy as jnp
from jax import lax
from jax.experimental import pallas as pl
from jax.experimental.pallas import tpu as pltpu
from jax.sharding import PartitionSpec as P

HEAD = 128
GROUP = 8
ROWS = 128
BACK = 6
SLOTS = BACK + 1
PAIRS = GROUP // 2
MESH = pl.DeviceIdType.MESH
NEG = -1e30
CONTRACT_LAST = (((1,), (1,)), ((), ()))


def near_of(g):
    return 4 if g % 2 == 0 else 3


def kernel(
    kv_heads, n_dp, n_seq,
    q_hbm, k_hbm, v_hbm, go_hbm, len_ref,
    dq_ref, dk_ref, dv_ref,
    q_ref, go_ref, kv, kt, bias, s_ref, g_ref, part, out_buf, in_buf,
    load_sem, own_sem, kv_send, kv_recv, d_send, d_recv,
):
    total = n_dp * n_seq
    me = lax.axis_index("dp") * n_seq + lax.axis_index("seq")

    def device(offset):
        there = lax.rem(me + (offset + total), total)
        return (there // n_seq, lax.rem(there, n_seq))

    own = []
    for g in range(kv_heads):
        for which, ref in ((0, k_hbm), (1, v_hbm)):
            own.append(pltpu.make_async_copy(
                ref.at[:, pl.ds(g * HEAD, HEAD)], kv.at[g, which, 0], own_sem.at[g, which]))
            own[-1].start()
    load_q = pltpu.make_async_copy(q_hbm, q_ref, load_sem.at[0])
    load_go = pltpu.make_async_copy(go_hbm, go_ref, load_sem.at[1])
    load_q.start()
    load_go.start()

    barrier = pltpu.get_barrier_semaphore()
    partners = (1, -1, BACK, -BACK)
    for offset in partners:
        pl.semaphore_signal(barrier, inc=1, device_id=device(offset), device_id_type=MESH)

    lens = len_ref[...].astype(jnp.float32)
    n_len = lens.shape[1]
    j = lax.broadcasted_iota(jnp.int32, (n_len, n_len), 0)
    k = lax.broadcasted_iota(jnp.int32, (n_len, n_len), 1)
    ends = jnp.sum(jnp.where(k <= j, jnp.broadcast_to(lens, (n_len, n_len)), 0.0), axis=1, keepdims=True)
    q_pos = (me * ROWS + lax.broadcasted_iota(jnp.int32, (1, ROWS), 1)).astype(jnp.float32)
    first = jnp.max(jnp.where(ends <= q_pos, ends, 0.0), axis=0, keepdims=True)
    for d in range(SLOTS):
        k_pos = ((me - d) * ROWS + lax.broadcasted_iota(jnp.int32, (ROWS, ROWS), 0)).astype(jnp.float32)
        bias[d] = jnp.where((k_pos >= first) & (k_pos <= q_pos), 0.0, NEG)
    part[...] = jnp.zeros_like(part)

    pl.semaphore_wait(barrier, len(partners))

    def kv_copy(g, source, target):
        offset = {(0, BACK): BACK}.get((source, target), target - source)
        return pltpu.make_async_remote_copy(
            src_ref=kv.at[g, :, source], dst_ref=kv.at[g, :, target],
            send_sem=kv_send.at[g, target], recv_sem=kv_recv.at[g, target],
            device_id=device(offset), device_id_type=MESH)

    def kv_first(g):
        own[2 * g].wait()
        own[2 * g + 1].wait()
        kv_copy(g, 0, 1).start()
        kv_copy(g, 0, BACK).start()

    def kv_pass(g, hop):
        near, far = hop, BACK + 1 - hop
        if near <= near_of(g):
            kv_copy(g, near - 1, near).wait_recv()
            if near < near_of(g):
                kv_copy(g, near, near + 1).start()
        if far > near_of(g):
            kv_copy(g, 0 if far == BACK else far + 1, far).wait_recv()
            if far - 1 > near_of(g):
                kv_copy(g, far, far - 1).start()

    def d_copy(g, source, target, offset):
        return pltpu.make_async_remote_copy(
            src_ref=out_buf.at[g, source], dst_ref=in_buf.at[g, target],
            send_sem=d_send.at[g, source], recv_sem=d_recv.at[g, target],
            device_id=device(offset), device_id_type=MESH)

    def d_near(g, d):
        return d_copy(g, d, d - 1, -1)

    def d_far(g, d):
        return d_copy(g, d, d + 1, 1 if d < BACK else -BACK)

    def d_first(g):
        for d, copy in ((near_of(g), d_near), (near_of(g) + 1, d_far)):
            out_buf[g, d] = part[g, :, d].astype(jnp.bfloat16)
            copy(g, d).start()

    def d_pass(g, hop):
        d = near_of(g) - hop
        if d >= 1:
            d_near(g, d + 1).wait_recv()
            out_buf[g, d] = (part[g, :, d] + in_buf[g, d].astype(jnp.float32)).astype(jnp.bfloat16)
            d_near(g, d).start()
        d = near_of(g) + 1 + hop
        if d <= BACK:
            d_far(g, d - 1).wait_recv()
            out_buf[g, d] = (part[g, :, d] + in_buf[g, d].astype(jnp.float32)).astype(jnp.bfloat16)
            d_far(g, d).start()
        if hop == near_of(g):
            d_near(g, 1).wait_recv()
            d_far(g, BACK).wait_recv()
            done = part[g, :, 0] + in_buf[g, 0].astype(jnp.float32) + in_buf[g, BACK + 1].astype(jnp.float32)
            dk_ref[:, g * HEAD:(g + 1) * HEAD] = done[0].astype(jnp.bfloat16)
            dv_ref[:, g * HEAD:(g + 1) * HEAD] = done[1].astype(jnp.bfloat16)

    scale = 1.0 / math.sqrt(HEAD)
    exp_scale = scale / math.log(2.0)

    def flat(x):
        return x.reshape(SLOTS * ROWS, x.shape[-1])

    def heads_of(ref, at):
        return jnp.concatenate([ref[:, pl.ds(at, HEAD)], ref[:, pl.ds(at + HEAD, HEAD)]], axis=0)

    def pair(g, p):
        at = pl.multiple_of((g * PAIRS + p) * (2 * HEAD), 2 * HEAD)

        @pl.when(p == 0)
        def _():
            kt[...] = flat(kv[g, 0]).T

        q2, go2 = heads_of(q_ref, at), heads_of(go_ref, at)
        keys, vals = flat(kv[g, 0]), flat(kv[g, 1])
        off = flat(bias[...])
        s = lax.dot_general(keys, q2, CONTRACT_LAST, preferred_element_type=jnp.float32)
        s = s + jnp.concatenate([off, off], axis=1)
        s_ref[...] = s
        top = jnp.max(s, axis=0, keepdims=True)
        grads = lax.dot_general(vals, go2, CONTRACT_LAST, preferred_element_type=jnp.float32)
        g_ref[...] = grads
        e = jnp.exp2((s_ref[...] - top) * exp_scale)
        s_ref[...] = e
        inv = 1.0 / jnp.sum(e, axis=0, keepdims=True)
        delta = jnp.sum(e * grads, axis=0, keepdims=True) * inv
        e = s_ref[...]
        low = (e * inv).astype(jnp.bfloat16)
        ds = ((e * (inv * scale)) * (g_ref[...] - delta)).astype(jnp.bfloat16)
        dk = jnp.dot(ds, q2, preferred_element_type=jnp.float32)
        dv = jnp.dot(low, go2, preferred_element_type=jnp.float32)
        part[g, 0] += dk.reshape(SLOTS, ROWS, HEAD)
        part[g, 1] += dv.reshape(SLOTS, ROWS, HEAD)
        dq = jnp.dot(kt[...], ds, preferred_element_type=jnp.float32).T.astype(jnp.bfloat16)
        dq_ref[:, pl.ds(at, HEAD)] = dq[:ROWS]
        dq_ref[:, pl.ds(at + HEAD, HEAD)] = dq[ROWS:]

    n = kv_heads * PAIRS
    events = [(-9, kv_first, (0,)), (-9, kv_first, (1,))]
    for g in range(2):
        for hop in range(1, near_of(g) + 1):
            events.append((-9 + hop if g == 0 else -9 + hop + 0.5, kv_pass, (g, hop)))
    events.append((-6.5, kv_first, (2,)))
    events.append((-5.5, kv_first, (3,)))
    for g in range(2, kv_heads):
        for hop in range(1, near_of(g) + 1):
            events.append((2 * hop - 2 + (g - 2), kv_pass, (g, hop)))
    for g in range(kv_heads):
        events.append((PAIRS * (g + 1), d_first, (g,)))
        for hop in range(1, near_of(g) + 1):
            events.append((PAIRS * (g + 1) + 2 * hop, d_pass, (g, hop)))
    events.sort(key=lambda event: event[0])
    for when, what, which in events:
        if when < 0:
            what(*which)
    load_q.wait()
    load_go.wait()

    def step(t, carry):
        for g in range(kv_heads):
            @pl.when(t // PAIRS == g)
            def _(g=g):
                for p in range(PAIRS):
                    now = [e for e in events if int(math.floor(e[0])) == g * PAIRS + p and e[0] >= 0]
                    if now:
                        @pl.when(lax.rem(t, PAIRS) == p)
                        def _(now=now):
                            for _, what, which in now:
                                what(*which)
        pair(t // PAIRS, lax.rem(t, PAIRS))
        return carry

    lax.fori_loop(0, n, step, 0)
    for when, what, which in events:
        if when >= n:
            what(*which)

    for g in range(kv_heads):
        for d in range(1, SLOTS):
            near = d <= near_of(g)
            kv_copy(g, d - 1 if near else (0 if d == BACK else d + 1), d).wait_send()
            (d_near if near else d_far)(g, d).wait_send()


def local(n_dp, n_seq, queries, keys, values, d_out, doc_lengths):
    rows, width = queries.shape
    kv_width = keys.shape[1]
    kv_heads = kv_width // HEAD
    padded = -(-doc_lengths.shape[0] // 128) * 128
    lens = jnp.pad(doc_lengths, (0, padded - doc_lengths.shape[0])).reshape(1, padded)
    anywhere, vmem = pl.BlockSpec(memory_space=pl.ANY), pl.BlockSpec(memory_space=pltpu.VMEM)
    dma = pltpu.SemaphoreType.DMA
    bf16, f32 = jnp.bfloat16, jnp.float32
    return pl.pallas_call(
        functools.partial(kernel, kv_heads, n_dp, n_seq),
        out_shape=(
            jax.ShapeDtypeStruct((rows, width), bf16),
            jax.ShapeDtypeStruct((rows, kv_width), bf16),
            jax.ShapeDtypeStruct((rows, kv_width), bf16),
        ),
        in_specs=[anywhere] * 4 + [vmem],
        out_specs=(vmem, vmem, vmem),
        scratch_shapes=[
            pltpu.VMEM((rows, width), bf16),
            pltpu.VMEM((rows, width), bf16),
            pltpu.VMEM((kv_heads, 2, SLOTS, ROWS, HEAD), bf16),
            pltpu.VMEM((HEAD, SLOTS * ROWS), bf16),
            pltpu.VMEM((SLOTS, ROWS, ROWS), f32),
            pltpu.VMEM((SLOTS * ROWS, 2 * ROWS), f32),
            pltpu.VMEM((SLOTS * ROWS, 2 * ROWS), f32),
            pltpu.VMEM((kv_heads, 2, SLOTS, ROWS, HEAD), f32),
            pltpu.VMEM((kv_heads, SLOTS, 2, ROWS, HEAD), bf16),
            pltpu.VMEM((kv_heads, SLOTS + 1, 2, ROWS, HEAD), bf16),
            dma((2,)),
            dma((kv_heads, 2)),
            dma((kv_heads, SLOTS)),
            dma((kv_heads, SLOTS)),
            dma((kv_heads, SLOTS)),
            dma((kv_heads, SLOTS + 1)),
        ],
        compiler_params=pltpu.CompilerParams(
            collective_id=0, has_side_effects=True, vmem_limit_bytes=48 * 2**20
        ),
        cost_estimate=pl.CostEstimate(flops=4_700_000_000, bytes_accessed=4_000_000, transcendentals=3_700_000),
    )(queries, keys, values, d_out, lens)


def solution(mesh):
    rows = P(("dp", "seq"), None)
    return jax.shard_map(
        functools.partial(local, mesh.shape["dp"], mesh.shape["seq"]),
        mesh=mesh, in_specs=(rows, rows, rows, rows, P()), out_specs=(rows, rows, rows), check_vma=False)
```

```python
import functools
import math

import jax
import jax.numpy as jnp
from jax import lax
from jax.experimental import pallas as pl
from jax.experimental.pallas import tpu as pltpu
from jax.sharding import PartitionSpec as P

HEAD = 128
GROUP = 8
ROWS = 128
BACK = 6
SLOTS = BACK + 1
PAIRS = GROUP // 2
MESH = pl.DeviceIdType.MESH
NEG = -1e30
CONTRACT_LAST = (((1,), (1,)), ((), ()))


NEAR = 3
SCHEDULE = (
    (("kf", 0), ("kf", 1), ("kn", 0, 1), ("kn", 1, 1), ("kx", 0, 6), ("kf", 2), ("kn", 0, 2), ("kx", 1, 6), ("kn", 1, 2), ("kx", 0, 5), ("kn", 2, 1), ("kn", 0, 3), ("kx", 2, 6), ("kn", 1, 3), ("kx", 1, 5), ("kf", 3), ("kn", 2, 2), ("kx", 0, 4),),
    (("kx", 2, 5),),
    (("kn", 3, 1),),
    (("kx", 1, 4), ("kn", 2, 3),),
    (("df", 0),),
    (),
    (("kx", 3, 6), ("kn", 3, 2), ("kx", 2, 4),),
    (),
    (("df", 1), ("dn", 0, 2), ("dx", 0, 5),),
    (("kx", 3, 5), ("kn", 3, 3),),
    (),
    (("dn", 1, 2), ("dx", 1, 5), ("dn", 0, 1), ("dx", 0, 6), ("kx", 3, 4),),
    (("df", 2), ("dn", 1, 1), ("dx", 1, 6),),
    (),
    (),
    (),
    (("df", 3), ("dd", 0), ("dn", 2, 2), ("dx", 2, 5), ("dd", 1), ("dn", 3, 2), ("dx", 3, 5), ("dn", 2, 1), ("dx", 2, 6), ("dn", 3, 1), ("dx", 3, 6), ("dd", 2), ("dd", 3),),
)


def kernel(
    kv_heads, n_dp, n_seq,
    q_hbm, k_hbm, v_hbm, go_hbm, len_ref,
    dq_ref, dk_ref, dv_ref,
    q_ref, go_ref, kv, kt, bias, s_a, g_a, top_a, s_b, g_b, top_b, part, out_buf, in_buf,
    load_sem, own_sem, kv_send, kv_recv, d_send, d_recv,
):
    total = n_dp * n_seq
    me = lax.axis_index("dp") * n_seq + lax.axis_index("seq")

    def device(offset):
        there = lax.rem(me + (offset + total), total)
        return (there // n_seq, lax.rem(there, n_seq))

    own = []
    for g in range(kv_heads):
        for which, ref in ((0, k_hbm), (1, v_hbm)):
            own.append(pltpu.make_async_copy(
                ref.at[:, pl.ds(g * HEAD, HEAD)], kv.at[g, 0, which], own_sem.at[g, which]))
            own[-1].start()
    load_q = pltpu.make_async_copy(q_hbm, q_ref, load_sem.at[0])
    load_go = pltpu.make_async_copy(go_hbm, go_ref, load_sem.at[1])
    load_q.start()
    load_go.start()

    barrier = pltpu.get_barrier_semaphore()
    partners = (1, -1, BACK, -BACK)
    for offset in partners:
        pl.semaphore_signal(barrier, inc=1, device_id=device(offset), device_id_type=MESH)

    pl.semaphore_wait(barrier, len(partners))

    def kv_copy(g, source, target):
        offset = {(0, BACK): BACK}.get((source, target), target - source)
        return pltpu.make_async_remote_copy(
            src_ref=kv.at[g, source], dst_ref=kv.at[g, target],
            send_sem=kv_send.at[g, target], recv_sem=kv_recv.at[g, target],
            device_id=device(offset), device_id_type=MESH)

    def kv_first(g):
        own[2 * g].wait()
        own[2 * g + 1].wait()
        kv_copy(g, 0, 1).start()
        kv_copy(g, 0, BACK).start()

    def kv_near(g, d):
        kv_copy(g, d - 1, d).wait_recv()
        if d < NEAR:
            kv_copy(g, d, d + 1).start()

    def kv_far(g, d):
        kv_copy(g, 0 if d == BACK else d + 1, d).wait_recv()
        if d > NEAR + 1:
            kv_copy(g, d, d - 1).start()

    def d_copy(g, source, target, offset):
        return pltpu.make_async_remote_copy(
            src_ref=out_buf.at[g, source], dst_ref=in_buf.at[g, target],
            send_sem=d_send.at[g, source], recv_sem=d_recv.at[g, target],
            device_id=device(offset), device_id_type=MESH)

    def d_near(g, d):
        return d_copy(g, d, d - 1, -1)

    def d_far(g, d):
        return d_copy(g, d, d + 1, 1 if d < BACK else -BACK)

    def d_first(g):
        for d, copy in ((NEAR, d_near), (NEAR + 1, d_far)):
            out_buf[g, d] = part[g, :, d].astype(jnp.bfloat16)
            copy(g, d).start()

    def add_on(g, d):
        out_buf[g, d] = (part[g, :, d] + in_buf[g, d].astype(jnp.float32)).astype(jnp.bfloat16)

    def d_pass_near(g, d):
        d_near(g, d + 1).wait_recv()
        add_on(g, d)
        d_near(g, d).start()

    def d_pass_far(g, d):
        d_far(g, d - 1).wait_recv()
        add_on(g, d)
        d_far(g, d).start()

    def d_done(g):
        d_near(g, 1).wait_recv()
        d_far(g, BACK).wait_recv()
        done = part[g, :, 0] + in_buf[g, 0].astype(jnp.float32) + in_buf[g, BACK + 1].astype(jnp.float32)
        dk_ref[:, g * HEAD:(g + 1) * HEAD] = done[0].astype(jnp.bfloat16)
        dv_ref[:, g * HEAD:(g + 1) * HEAD] = done[1].astype(jnp.bfloat16)

    acts = {"kf": kv_first, "kn": kv_near, "kx": kv_far,
            "df": d_first, "dn": d_pass_near, "dx": d_pass_far, "dd": d_done}

    def act(slot):
        for kind, *which in slot:
            acts[kind](*which)

    scale = 1.0 / math.sqrt(HEAD)
    exp_scale = scale / math.log(2.0)

    def flat(x):
        return x.reshape(SLOTS * ROWS, x.shape[-1])

    def heads_of(ref, at):
        return jnp.concatenate([ref[:, pl.ds(at, HEAD)], ref[:, pl.ds(at + HEAD, HEAD)]], axis=0)

    def place(t):
        return t // PAIRS, pl.multiple_of(t * (2 * HEAD), 2 * HEAD)

    def products(t, s_ref, g_ref, top_ref):
        g, at = place(t)
        off = flat(bias[...])
        s = lax.dot_general(flat(kv[g, :, 0]), heads_of(q_ref, at), CONTRACT_LAST, preferred_element_type=jnp.float32)
        s = s + jnp.concatenate([off, off], axis=1)
        s_ref[...] = s
        top_ref[...] = jnp.max(s, axis=0, keepdims=True)
        g_ref[...] = lax.dot_general(
            flat(kv[g, :, 1]), heads_of(go_ref, at), CONTRACT_LAST, preferred_element_type=jnp.float32)

    def finish(t, s_ref, g_ref, top_ref):
        g, at = place(t)
        q2, go2 = heads_of(q_ref, at), heads_of(go_ref, at)
        e = jnp.exp2((s_ref[...] - top_ref[...]) * exp_scale)
        s_ref[...] = e
        inv = 1.0 / jnp.sum(e, axis=0, keepdims=True)
        delta = jnp.sum(e * g_ref[...], axis=0, keepdims=True) * inv
        e = s_ref[...]
        low = (e * inv).astype(jnp.bfloat16)
        ds = ((e * (inv * scale)) * (g_ref[...] - delta)).astype(jnp.bfloat16)
        dk = jnp.dot(ds, q2, preferred_element_type=jnp.float32)
        dv = jnp.dot(low, go2, preferred_element_type=jnp.float32)
        part[g, 0] += dk.reshape(SLOTS, ROWS, HEAD)
        part[g, 1] += dv.reshape(SLOTS, ROWS, HEAD)
        dq = jnp.dot(kt[g], ds, preferred_element_type=jnp.float32).T.astype(jnp.bfloat16)
        dq_ref[:, pl.ds(at, HEAD)] = dq[:ROWS]
        dq_ref[:, pl.ds(at + HEAD, HEAD)] = dq[ROWS:]

    starts = 0
    while SCHEDULE[0][starts][0] == "kf":
        starts += 1
    act(SCHEDULE[0][:starts])

    lens = len_ref[...].astype(jnp.float32)
    n_len = lens.shape[1]
    j = lax.broadcasted_iota(jnp.int32, (n_len, n_len), 0)
    k = lax.broadcasted_iota(jnp.int32, (n_len, n_len), 1)
    ends = jnp.sum(jnp.where(k <= j, jnp.broadcast_to(lens, (n_len, n_len)), 0.0), axis=1, keepdims=True)
    q_pos = (me * ROWS + lax.broadcasted_iota(jnp.int32, (1, ROWS), 1)).astype(jnp.float32)
    first = jnp.max(jnp.where(ends <= q_pos, ends, 0.0), axis=0, keepdims=True)
    for d in range(SLOTS):
        k_pos = ((me - d) * ROWS + lax.broadcasted_iota(jnp.int32, (ROWS, ROWS), 0)).astype(jnp.float32)
        bias[d] = jnp.where((k_pos >= first) & (k_pos <= q_pos), 0.0, NEG)
    part[...] = jnp.zeros_like(part)

    act(SCHEDULE[0][starts:])
    load_q.wait()
    load_go.wait()

    held = ((s_a, g_a, top_a), (s_b, g_b, top_b))
    n = kv_heads * PAIRS

    def events_of(t, parity):
        for p in range(parity, n, 2):
            if p and SCHEDULE[p]:
                @pl.when(t == p)
                def _(p=p):
                    act(SCHEDULE[p])

    def turn_keys(t):
        @pl.when(lax.rem(t, PAIRS) == 0)
        def _():
            kt[t // PAIRS] = flat(kv[t // PAIRS, :, 0]).T

    def step(u, carry):
        t = 2 * u
        events_of(t, 0)
        products(t + 1, *held[1])
        finish(t, *held[0])
        events_of(t + 1, 1)

        @pl.when(t + 2 < n)
        def _():
            turn_keys(t + 2)

        products(jnp.minimum(t + 2, n - 1), *held[0])
        finish(t + 1, *held[1])
        return carry

    turn_keys(0)
    products(0, *held[0])
    lax.fori_loop(0, n // 2, step, 0)
    act(SCHEDULE[-1])

    for g in range(kv_heads):
        for d in range(1, SLOTS):
            kv_copy(g, d - 1 if d <= NEAR else (0 if d == BACK else d + 1), d).wait_send()
            (d_near if d <= NEAR else d_far)(g, d).wait_send()


def write_out(a_ref, b_ref, c_ref, a_out, b_out, c_out, sem):
    pairs = ((a_ref, a_out), (b_ref, b_out), (c_ref, c_out))
    copies = [pltpu.make_async_copy(x, y, sem.at[i]) for i, (x, y) in enumerate(pairs)]
    for copy in copies:
        copy.start()
    for copy in copies:
        copy.wait()


def local(n_dp, n_seq, queries, keys, values, d_out, doc_lengths):
    rows, width = queries.shape
    kv_width = keys.shape[1]
    kv_heads = kv_width // HEAD
    lens = doc_lengths.reshape(1, -1)
    hbm, vmem = pl.BlockSpec(memory_space=pltpu.HBM), pl.BlockSpec(memory_space=pltpu.VMEM)
    dma = pltpu.SemaphoreType.DMA
    bf16, f32 = jnp.bfloat16, jnp.float32
    held = (
        pltpu.VMEM((SLOTS * ROWS, 2 * ROWS), f32),
        pltpu.VMEM((SLOTS * ROWS, 2 * ROWS), f32),
        pltpu.VMEM((1, 2 * ROWS), f32),
    )
    outs = (
        jax.ShapeDtypeStruct((rows, width), bf16),
        jax.ShapeDtypeStruct((rows, kv_width), bf16),
        jax.ShapeDtypeStruct((rows, kv_width), bf16),
    )
    made = pl.pallas_call(
        functools.partial(kernel, kv_heads, n_dp, n_seq),
        out_shape=outs,
        in_specs=[hbm] * 4 + [vmem],
        out_specs=(vmem, vmem, vmem),
        scratch_shapes=[
            pltpu.VMEM((rows, width), bf16),
            pltpu.VMEM((rows, width), bf16),
            pltpu.VMEM((kv_heads, SLOTS, 2, ROWS, HEAD), bf16),
            pltpu.VMEM((kv_heads, HEAD, SLOTS * ROWS), bf16),
            pltpu.VMEM((SLOTS, ROWS, ROWS), f32),
            *held,
            *held,
            pltpu.VMEM((kv_heads, 2, SLOTS, ROWS, HEAD), f32),
            pltpu.VMEM((kv_heads, SLOTS, 2, ROWS, HEAD), bf16),
            pltpu.VMEM((kv_heads, SLOTS + 1, 2, ROWS, HEAD), bf16),
            dma((2,)),
            dma((kv_heads, 2)),
            dma((kv_heads, SLOTS)),
            dma((kv_heads, SLOTS)),
            dma((kv_heads, SLOTS)),
            dma((kv_heads, SLOTS + 1)),
        ],
        compiler_params=pltpu.CompilerParams(
            collective_id=0, has_side_effects=True, vmem_limit_bytes=40 * 2**20
        ),
        cost_estimate=pl.CostEstimate(flops=4_700_000_000, bytes_accessed=4_000_000, transcendentals=3_700_000),
    )(*(pltpu.with_memory_space_constraint(x, pltpu.HBM) for x in (queries, keys, values, d_out)), lens)
    return pl.pallas_call(
        write_out,
        out_shape=outs,
        in_specs=[vmem] * 3,
        out_specs=(hbm,) * 3,
        scratch_shapes=[dma((3,))],
        compiler_params=pltpu.CompilerParams(vmem_limit_bytes=4 * 2**20),
    )(*made)


def solution(mesh):
    rows = P(("dp", "seq"), None)
    return jax.shard_map(
        functools.partial(local, mesh.shape["dp"], mesh.shape["seq"]),
        mesh=mesh, in_specs=(rows, rows, rows, rows, P()), out_specs=(rows, rows, rows), check_vma=False)
```

```python
import functools
import math

import jax
import jax.numpy as jnp
from jax import lax
from jax.experimental import pallas as pl
from jax.experimental.pallas import tpu as pltpu
from jax.sharding import PartitionSpec as P

HEAD = 128
GROUP = 8
ROWS = 128
BACK = 6
SLOTS = BACK + 1
PAIRS = GROUP // 2
MESH = pl.DeviceIdType.MESH
NEG = -1e30
CONTRACT_LAST = (((1,), (1,)), ((), ()))


KV_FROM = (
    (0, 1, 0, 3, 6, 0),
    (0, 1, 2, 5, 6, 0),
    (0, 1, 2, 5, 6, 0),
    (0, 1, 2, 5, 6, 0),
)
NEAR_D = (4, 4, 3, 3)
SCHEDULE = (
    (("kf", 0), ("kf", 1), ("kf", 2), ("kv", 0, 1), ("kv", 0, 6), ("kv", 1, 6), ("kv", 0, 3), ("kv", 1, 1), ("kv", 2, 1), ("kv", 2, 6), ("kv", 0, 2), ("kv", 0, 5), ("kf", 3), ("kv", 1, 5), ("kv", 0, 4),),
    (("kv", 1, 2), ("kv", 2, 5),),
    (("kv", 2, 2),),
    (("kv", 3, 1), ("kv", 3, 6), ("kv", 1, 3), ("kv", 1, 4),),
    (("df", 0), ("kv", 2, 3), ("kv", 2, 4),),
    (("kv", 3, 2),),
    (("kv", 3, 5),),
    (),
    (("df", 1), ("dn", 0, 3), ("dx", 0, 6), ("kv", 3, 3),),
    (("kv", 3, 4),),
    (),
    (("dn", 1, 3), ("dx", 1, 6),),
    (("df", 2), ("dn", 0, 2),),
    (),
    (("dn", 1, 2),),
    (),
    (("df", 3), ("dn", 2, 2), ("dn", 0, 1), ("dx", 2, 5), ("dn", 1, 1), ("dn", 3, 2), ("dx", 3, 5), ("dn", 2, 1), ("dx", 2, 6), ("dd", 0), ("dd", 1), ("dx", 3, 6), ("dn", 3, 1), ("dd", 2), ("dd", 3),),
)


def kernel(
    kv_heads, n_dp, n_seq,
    q_hbm, k_hbm, v_hbm, go_hbm, len_hbm,
    dq_ref, dk_ref, dv_ref,
    q_ref, go_ref, len_ref, kv, kt, bias, s_a, g_a, top_a, s_b, g_b, top_b, part, out_buf, in_buf,
    load_sem, own_sem, kv_send, kv_recv, d_send, d_recv,
):
    total = n_dp * n_seq
    me = lax.axis_index("dp") * n_seq + lax.axis_index("seq")

    def device(offset):
        there = lax.rem(me + (offset + total), total)
        return (there // n_seq, lax.rem(there, n_seq))

    barrier = pltpu.get_barrier_semaphore()
    hops = {1, BACK}
    for source in KV_FROM:
        hops |= {abs(d - s) for d, s in zip(range(1, SLOTS), source)}
    partners = sorted(hops | {-hop for hop in hops})
    for offset in partners:
        pl.semaphore_signal(barrier, inc=1, device_id=device(offset), device_id_type=MESH)

    own = []
    for g in range(kv_heads):
        for which, ref in ((0, k_hbm), (1, v_hbm)):
            own.append(pltpu.make_async_copy(
                ref.at[:, pl.ds(g * HEAD, HEAD)], kv.at[g, 0, which], own_sem.at[g, which]))
            own[-1].start()
    load_q = pltpu.make_async_copy(q_hbm, q_ref, load_sem.at[0])
    load_go = pltpu.make_async_copy(go_hbm, go_ref, load_sem.at[1])
    load_len = pltpu.make_async_copy(len_hbm, len_ref, load_sem.at[2])
    load_len.start()
    load_q.start()
    load_go.start()

    pl.semaphore_wait(barrier, len(partners))

    def kv_copy(g, source, target):
        offset = {(0, BACK): BACK}.get((source, target), target - source)
        return pltpu.make_async_remote_copy(
            src_ref=kv.at[g, source], dst_ref=kv.at[g, target],
            send_sem=kv_send.at[g, target], recv_sem=kv_recv.at[g, target],
            device_id=device(offset), device_id_type=MESH)

    def kv_pass(g, source):
        for d in range(1, SLOTS):
            if KV_FROM[g][d - 1] == source:
                kv_copy(g, source, d).start()

    def kv_first(g):
        own[2 * g].wait()
        own[2 * g + 1].wait()
        kv_pass(g, 0)

    def kv_take(g, d):
        kv_copy(g, KV_FROM[g][d - 1], d).wait_recv()
        kv_pass(g, d)

    def d_copy(g, source, target, offset):
        return pltpu.make_async_remote_copy(
            src_ref=out_buf.at[g, source], dst_ref=in_buf.at[g, target],
            send_sem=d_send.at[g, source], recv_sem=d_recv.at[g, target],
            device_id=device(offset), device_id_type=MESH)

    def d_near(g, d):
        return d_copy(g, d, d - 1, -1)

    def d_far(g, d):
        return d_copy(g, d, d + 1, 1 if d < BACK else -BACK)

    def d_first(g):
        for d, copy in ((NEAR_D[g], d_near), (NEAR_D[g] + 1, d_far)):
            out_buf[g, d] = part[g, :, d].astype(jnp.bfloat16)
            copy(g, d).start()

    def add_on(g, d):
        out_buf[g, d] = (part[g, :, d] + in_buf[g, d].astype(jnp.float32)).astype(jnp.bfloat16)

    def d_pass_near(g, d):
        d_near(g, d + 1).wait_recv()
        add_on(g, d)
        d_near(g, d).start()

    def d_pass_far(g, d):
        d_far(g, d - 1).wait_recv()
        add_on(g, d)
        d_far(g, d).start()

    def d_done(g):
        d_near(g, 1).wait_recv()
        d_far(g, BACK).wait_recv()
        done = part[g, :, 0] + in_buf[g, 0].astype(jnp.float32) + in_buf[g, BACK + 1].astype(jnp.float32)
        dk_ref[:, g * HEAD:(g + 1) * HEAD] = done[0].astype(jnp.bfloat16)
        dv_ref[:, g * HEAD:(g + 1) * HEAD] = done[1].astype(jnp.bfloat16)

    acts = {"kf": kv_first, "kv": kv_take,
            "df": d_first, "dn": d_pass_near, "dx": d_pass_far, "dd": d_done}

    def act(slot):
        for kind, *which in slot:
            acts[kind](*which)

    scale = 1.0 / math.sqrt(HEAD)
    exp_scale = scale / math.log(2.0)

    def flat(x):
        return x.reshape(SLOTS * ROWS, x.shape[-1])

    def heads_of(ref, at):
        return jnp.concatenate([ref[:, pl.ds(at, HEAD)], ref[:, pl.ds(at + HEAD, HEAD)]], axis=0)

    def place(t):
        return t // PAIRS, pl.multiple_of(t * (2 * HEAD), 2 * HEAD)

    def products(t, s_ref, g_ref, top_ref):
        g, at = place(t)
        off = flat(bias[...])
        s = lax.dot_general(flat(kv[g, :, 0]), heads_of(q_ref, at), CONTRACT_LAST, preferred_element_type=jnp.float32)
        s = s + jnp.concatenate([off, off], axis=1)
        s_ref[...] = s
        top_ref[...] = jnp.max(s, axis=0, keepdims=True)
        g_ref[...] = lax.dot_general(
            flat(kv[g, :, 1]), heads_of(go_ref, at), CONTRACT_LAST, preferred_element_type=jnp.float32)

    def finish(t, s_ref, g_ref, top_ref):
        g, at = place(t)
        q2, go2 = heads_of(q_ref, at), heads_of(go_ref, at)
        e = jnp.exp2((s_ref[...] - top_ref[...]) * exp_scale)
        s_ref[...] = e
        inv = 1.0 / jnp.sum(e, axis=0, keepdims=True)
        delta = jnp.sum(e * g_ref[...], axis=0, keepdims=True) * inv
        e = s_ref[...]
        low = (e * inv).astype(jnp.bfloat16)
        ds = ((e * (inv * scale)) * (g_ref[...] - delta)).astype(jnp.bfloat16)
        dk = jnp.dot(ds, q2, preferred_element_type=jnp.float32)
        dv = jnp.dot(low, go2, preferred_element_type=jnp.float32)
        part[g, 0] += dk.reshape(SLOTS, ROWS, HEAD)
        part[g, 1] += dv.reshape(SLOTS, ROWS, HEAD)
        dq = jnp.dot(kt[g], ds, preferred_element_type=jnp.float32).T.astype(jnp.bfloat16)
        dq_ref[:, pl.ds(at, HEAD)] = dq[:ROWS]
        dq_ref[:, pl.ds(at + HEAD, HEAD)] = dq[ROWS:]

    starts = 0
    while SCHEDULE[0][starts][0] == "kf":
        starts += 1
    act(SCHEDULE[0][:starts])

    load_len.wait()
    lens = len_ref[...].astype(jnp.float32)
    n_len = lens.shape[1]
    j = lax.broadcasted_iota(jnp.int32, (n_len, n_len), 0)
    k = lax.broadcasted_iota(jnp.int32, (n_len, n_len), 1)
    ends = jnp.sum(jnp.where(k <= j, jnp.broadcast_to(lens, (n_len, n_len)), 0.0), axis=1, keepdims=True)
    q_pos = (me * ROWS + lax.broadcasted_iota(jnp.int32, (1, ROWS), 1)).astype(jnp.float32)
    first = jnp.max(jnp.where(ends <= q_pos, ends, 0.0), axis=0, keepdims=True)
    for d in range(SLOTS):
        k_pos = ((me - d) * ROWS + lax.broadcasted_iota(jnp.int32, (ROWS, ROWS), 0)).astype(jnp.float32)
        bias[d] = jnp.where((k_pos >= first) & (k_pos <= q_pos), 0.0, NEG)
    part[...] = jnp.zeros_like(part)

    act(SCHEDULE[0][starts:])
    load_q.wait()
    load_go.wait()

    held = ((s_a, g_a, top_a), (s_b, g_b, top_b))
    n = kv_heads * PAIRS

    def events_of(t, parity):
        for p in range(parity, n, 2):
            if p and SCHEDULE[p]:
                @pl.when(t == p)
                def _(p=p):
                    act(SCHEDULE[p])

    def turn_keys(t):
        @pl.when(lax.rem(t, PAIRS) == 0)
        def _():
            kt[t // PAIRS] = flat(kv[t // PAIRS, :, 0]).T

    def step(u, carry):
        t = 2 * u
        events_of(t, 0)
        products(t + 1, *held[1])
        finish(t, *held[0])
        events_of(t + 1, 1)

        @pl.when(t + 2 < n)
        def _():
            turn_keys(t + 2)

        products(jnp.minimum(t + 2, n - 1), *held[0])
        finish(t + 1, *held[1])
        return carry

    turn_keys(0)
    products(0, *held[0])
    lax.fori_loop(0, n // 2, step, 0)
    act(SCHEDULE[-1])

    for g in range(kv_heads):
        for d in range(1, SLOTS):
            kv_copy(g, KV_FROM[g][d - 1], d).wait_send()
            (d_near if d <= NEAR_D[g] else d_far)(g, d).wait_send()


def write_out(a_ref, b_ref, c_ref, a_out, b_out, c_out, sem):
    pairs = ((a_ref, a_out), (b_ref, b_out), (c_ref, c_out))
    copies = [pltpu.make_async_copy(x, y, sem.at[i]) for i, (x, y) in enumerate(pairs)]
    for copy in copies:
        copy.start()
    for copy in copies:
        copy.wait()


def local(n_dp, n_seq, queries, keys, values, d_out, doc_lengths):
    rows, width = queries.shape
    kv_width = keys.shape[1]
    kv_heads = kv_width // HEAD
    lens = doc_lengths.reshape(1, -1)
    hbm, vmem = pl.BlockSpec(memory_space=pltpu.HBM), pl.BlockSpec(memory_space=pltpu.VMEM)
    dma = pltpu.SemaphoreType.DMA
    bf16, f32 = jnp.bfloat16, jnp.float32
    held = (
        pltpu.VMEM((SLOTS * ROWS, 2 * ROWS), f32),
        pltpu.VMEM((SLOTS * ROWS, 2 * ROWS), f32),
        pltpu.VMEM((1, 2 * ROWS), f32),
    )
    outs = (
        jax.ShapeDtypeStruct((rows, width), bf16),
        jax.ShapeDtypeStruct((rows, kv_width), bf16),
        jax.ShapeDtypeStruct((rows, kv_width), bf16),
    )
    made = pl.pallas_call(
        functools.partial(kernel, kv_heads, n_dp, n_seq),
        out_shape=outs,
        in_specs=[hbm] * 5,
        out_specs=(vmem, vmem, vmem),
        scratch_shapes=[
            pltpu.VMEM((rows, width), bf16),
            pltpu.VMEM((rows, width), bf16),
            pltpu.VMEM(lens.shape, jnp.int32),
            pltpu.VMEM((kv_heads, SLOTS, 2, ROWS, HEAD), bf16),
            pltpu.VMEM((kv_heads, HEAD, SLOTS * ROWS), bf16),
            pltpu.VMEM((SLOTS, ROWS, ROWS), f32),
            *held,
            *held,
            pltpu.VMEM((kv_heads, 2, SLOTS, ROWS, HEAD), f32),
            pltpu.VMEM((kv_heads, SLOTS, 2, ROWS, HEAD), bf16),
            pltpu.VMEM((kv_heads, SLOTS + 1, 2, ROWS, HEAD), bf16),
            dma((3,)),
            dma((kv_heads, 2)),
            dma((kv_heads, SLOTS)),
            dma((kv_heads, SLOTS)),
            dma((kv_heads, SLOTS)),
            dma((kv_heads, SLOTS + 1)),
        ],
        compiler_params=pltpu.CompilerParams(
            collective_id=0, has_side_effects=True, vmem_limit_bytes=40 * 2**20
        ),
        cost_estimate=pl.CostEstimate(flops=4_700_000_000, bytes_accessed=4_000_000, transcendentals=3_700_000),
    )(*(pltpu.with_memory_space_constraint(x, pltpu.HBM) for x in (queries, keys, values, d_out, lens)))
    return pl.pallas_call(
        write_out,
        out_shape=outs,
        in_specs=[vmem] * 3,
        out_specs=(hbm,) * 3,
        scratch_shapes=[dma((3,))],
        compiler_params=pltpu.CompilerParams(vmem_limit_bytes=4 * 2**20),
    )(*made)


def solution(mesh):
    rows = P(("dp", "seq"), None)
    return jax.shard_map(
        functools.partial(local, mesh.shape["dp"], mesh.shape["seq"]),
        mesh=mesh, in_specs=(rows, rows, rows, rows, P()), out_specs=(rows, rows, rows), check_vma=False)
```
